32 devices in a mesh: shard: 2 (over y), context: 8 (over z, x), tensor: 2 (over core).
Axes of the slice: x: 2, y: 2, z: 4, core: 2. Of those that a mesh axis runs over, the one named last changes fastest.
Arguments:
- tokens: bfloat16 [2, 2048, 960], P('shard', ('context', 'tensor')), may hold values from -6 to 6
- positions: int32 [2, 2048], P('shard', ('context', 'tensor')), may hold values from 0 to 2047, as said below
- gain_one: float32 [960], replicated, may hold values from 0.5 to 1.5
- w_query: bfloat16 [960, 960], P(('context', 'tensor'), 'shard'), may hold values from -0.1875 to 0.1875
- key_weight: bfloat16 [320, 960], P(('context', 'tensor'), 'shard'), may hold values from -0.1875 to 0.1875
- value_weight: bfloat16 [320, 960], P(('context', 'tensor'), 'shard'), may hold values from -0.1875 to 0.1875
- w_out: bfloat16 [960, 960], P(('context', 'tensor'), 'shard'), may hold values from -6 to 6
- gain_two: float32 [960], replicated, may hold values from 0.5 to 1.5
- w_gate: bfloat16 [2560, 960], P(('context', 'tensor'), 'shard'), may hold values from -0.1875 to 0.1875
- w_up: bfloat16 [2560, 960], P(('context', 'tensor'), 'shard'), may hold values from -0.1875 to 0.1875
- w_down: bfloat16 [2560, 960], P(('context', 'tensor'), 'shard'), may hold values from -0.125 to 0.125
- cotangent: bfloat16 [2, 2048, 960], P('shard', ('context', 'tensor')), may hold values from -6 to 6
Outputs:
- output: bfloat16 [2, 2048, 960], P('shard', ('context', 'tensor'))
- grad_tokens: bfloat16 [2, 2048, 960], P('shard', ('context', 'tensor'))
- grad_gain_one: float32 [960], replicated
- grad_w_query: float32 [960, 960], P(('context', 'tensor'), 'shard')
- grad_w_key: float32 [320, 960], P(('context', 'tensor'), 'shard')
- grad_w_value: float32 [320, 960], P(('context', 'tensor'), 'shard')
- grad_w_out: float32 [960, 960], P(('context', 'tensor'), 'shard')
- grad_gain_two: float32 [960], replicated
- grad_w_gate: float32 [2560, 960], P(('context', 'tensor'), 'shard')
- grad_w_up: float32 [2560, 960], P(('context', 'tensor'), 'shard')
- grad_w_down: float32 [2560, 960], P(('context', 'tensor'), 'shard')
The draws below stay inside these ranges and needn't reach their ends.
Inputs may be any that keep to these rules, and one draw needn't show every extreme that they name: In each sequence the positions are a permutation of 0 to 2047, and each aligned block of 128 rows (the rows of one device) holds consecutive increasing positions.
All inputs are finite; a program needn't handle non-finite values.
Results may differ from the reference program's by a relative error of at most 0.024.
Values may be sent and summed in bfloat16 or wider, within the bound.
A program may use at most 128 MiB of HBM per device.

```python
import math
import jax
import jax.numpy as jnp
from jax import lax

MODEL_WIDTH = 960
QUERY_HEAD_COUNT = 15
KEY_VALUE_HEADS = 5
HEAD_WIDTH = 64
FF = 2560
TOK_DEV = 128
SEQUENCE_LENGTH = 2048
SEQS = 2


def draw_positions(key, part):
    key = jax.random.fold_in(key, 11)
    block_count = SEQUENCE_LENGTH // TOK_DEV
    seq_keys = jax.random.split(key, SEQS)
    orders = jax.vmap(lambda seq_key: jax.random.permutation(seq_key, block_count))(seq_keys)
    offsets = jnp.arange(TOK_DEV, dtype=jnp.int32)
    slot_positions = orders.astype(jnp.int32)[:, :, None] * TOK_DEV + offsets[None, None, :]
    return slot_positions.reshape(SEQS, SEQUENCE_LENGTH).astype(jnp.int32)


def level_of(stream_key, extent, cuts, low, top_value):
    loudness, own = 1.0, jax.random.fold_in(stream_key, 6)
    for axis_at, parts in cuts:
        draws = jnp.exp(jax.random.uniform(jax.random.fold_in(own, axis_at), (parts,), jnp.float32, low / len(cuts), top_value / len(cuts)))
        loudness = loudness * jnp.repeat(draws, extent[axis_at] // parts).reshape([-1 if axis == axis_at else 1 for axis in range(len(extent))])
    return loudness


def centred(own_key, extent, width, bound, cuts=(), kind=jnp.bfloat16):
    level = level_of(own_key, extent, cuts, -0.22, 0.18) if cuts else 1.0
    drawn = jax.random.normal(own_key, extent, jnp.float32) * width * level
    return jnp.minimum(jnp.maximum(drawn, -bound), bound).astype(kind)


def setup_inputs(seed: int = 0) -> dict:
    arg_keys = jax.random.split(jax.random.key(seed), 13)
    return {
        "tokens": centred(arg_keys[0], (SEQS, SEQUENCE_LENGTH, MODEL_WIDTH), 1.0, 6.0, ((0, 2), (1, 16))),
        "positions": draw_positions(jax.random.fold_in(arg_keys[12], 71), 0),
        "gain_one": jnp.clip(1.0 + 0.1 * jax.random.normal(arg_keys[2], (MODEL_WIDTH,), jnp.float32), 0.5, 1.5),
        "w_query": centred(arg_keys[3], (QUERY_HEAD_COUNT * HEAD_WIDTH, MODEL_WIDTH), MODEL_WIDTH ** -0.5, 0.1875, ((0, 16), (1, 2))),
        "key_weight": centred(arg_keys[4], (KEY_VALUE_HEADS * HEAD_WIDTH, MODEL_WIDTH), MODEL_WIDTH ** -0.5, 0.1875, ((0, 16), (1, 2))),
        "value_weight": centred(arg_keys[5], (KEY_VALUE_HEADS * HEAD_WIDTH, MODEL_WIDTH), MODEL_WIDTH ** -0.5, 0.1875, ((0, 16), (1, 2))),
        "w_out": centred(arg_keys[6], (MODEL_WIDTH, QUERY_HEAD_COUNT * HEAD_WIDTH), (max(1, MODEL_WIDTH * 4 // SEQUENCE_LENGTH)) ** -0.5, 6.0, ((0, 16), (1, 2))),
        "gain_two": jnp.clip(1.0 + 0.1 * jax.random.normal(arg_keys[7], (MODEL_WIDTH,), jnp.float32), 0.5, 1.5),
        "w_gate": centred(arg_keys[8], (FF, MODEL_WIDTH), MODEL_WIDTH ** -0.5, 0.1875, ((0, 16), (1, 2))),
        "w_up": centred(arg_keys[9], (FF, MODEL_WIDTH), MODEL_WIDTH ** -0.5, 0.1875, ((0, 16), (1, 2))),
        "w_down": centred(arg_keys[10], (FF, MODEL_WIDTH), FF ** -0.5, 0.125, ((0, 16), (1, 2))),
        "cotangent": centred(arg_keys[11], (SEQS, SEQUENCE_LENGTH, MODEL_WIDTH), 1.0, 6.0, ((0, 2), (1, 16))),
    }


@jax.custom_vjp
def lower_precision(v):
    return lax.optimization_barrier(v.astype(jnp.bfloat16)).astype(jnp.float32)

@jax.custom_vjp
def low_back(v):
    return v

def low_keep(v):
    return (lower_precision(v), None)

def low_pass(kept, grad):
    return (grad,)

def back_keep(v):
    return (v, None)

def back_low(kept, grad):
    return (lower_precision(grad),)
lower_precision.defvjp(low_keep, low_pass)
low_back.defvjp(back_keep, back_low)
epsilon = 1e-05
highest = lax.Precision.HIGHEST

def rms_scale(value_matrix, gain):
    return value_matrix * lax.rsqrt(lax.optimization_barrier(jnp.mean(value_matrix * value_matrix, axis=-1, keepdims=True)) + epsilon) * gain

def apply_rotation(value_matrix, slot_positions, heads):
    half_dim = HEAD_WIDTH // 2
    freqs = 10000.0 ** (-jnp.arange(half_dim, dtype=jnp.float32) / half_dim)
    angles = slot_positions.astype(jnp.float32)[:, None] * freqs[None, :]
    cosine = jnp.cos(angles)[:, None, :]
    sine = jnp.sin(angles)[:, None, :]
    split_heads = value_matrix.reshape(value_matrix.shape[0], heads, HEAD_WIDTH)
    first_half = split_heads[..., :half_dim]
    second_half = split_heads[..., half_dim:]
    turned = jnp.concatenate([first_half * cosine - second_half * sine, second_half * cosine + first_half * sine], axis=-1)
    return turned.reshape(value_matrix.shape)

def attend(rotated_queries, rotated_keys, value_matrix, slot_positions):
    group_width = QUERY_HEAD_COUNT // KEY_VALUE_HEADS
    rows_per_block = math.gcd(SEQUENCE_LENGTH, 512)
    heads_of_keys = rotated_keys.reshape(SEQUENCE_LENGTH, KEY_VALUE_HEADS, HEAD_WIDTH)
    heads_of_values = value_matrix.reshape(SEQUENCE_LENGTH, KEY_VALUE_HEADS, HEAD_WIDTH)
    score_scale = HEAD_WIDTH ** (-0.5)

    def one_block(element):
        query_portion, query_places = element
        heads_of_queries = query_portion.reshape(rows_per_block, KEY_VALUE_HEADS, group_width, HEAD_WIDTH)
        scores = jnp.einsum('ikgd,jkd->kgij', heads_of_queries, heads_of_keys, precision=highest) * score_scale
        scores = low_back(scores)
        allowed = slot_positions[None, None, None, :] <= query_places[None, None, :, None]
        scores = jnp.where(allowed, scores, -1e+30)
        probs = lower_precision(jax.nn.softmax(scores, axis=-1))
        mixed = jnp.einsum('kgij,jkd->ikgd', probs, heads_of_values, precision=highest)
        return mixed.reshape(rows_per_block, QUERY_HEAD_COUNT * HEAD_WIDTH)
    blocks = (rotated_queries.reshape(SEQUENCE_LENGTH // rows_per_block, rows_per_block, QUERY_HEAD_COUNT * HEAD_WIDTH), slot_positions.reshape(SEQUENCE_LENGTH // rows_per_block, rows_per_block))
    result = lax.map(jax.checkpoint(one_block), blocks)
    return result.reshape(SEQUENCE_LENGTH, QUERY_HEAD_COUNT * HEAD_WIDTH)

def layer(inputs, gain_one, w_query, key_weight, value_weight, w_out, gain_two, w_gate, w_up, w_down, slot_positions):
    normed_one = lower_precision(rms_scale(inputs, gain_one))
    queries = low_back(jnp.dot(normed_one, w_query.T, precision=highest))
    key_matrix = low_back(jnp.dot(normed_one, key_weight.T, precision=highest))
    value_matrix = lower_precision(low_back(jnp.dot(normed_one, value_weight.T, precision=highest)))
    rotated_queries = lower_precision(apply_rotation(queries, slot_positions, QUERY_HEAD_COUNT))
    rotated_keys = lower_precision(apply_rotation(key_matrix, slot_positions, KEY_VALUE_HEADS))
    mixed = lower_precision(low_back(attend(rotated_queries, rotated_keys, value_matrix, slot_positions)))
    branch = low_back(jnp.dot(mixed, w_out.T, precision=highest))
    middle = inputs + branch
    normed_two = lower_precision(rms_scale(middle, gain_two))
    gates = low_back(jnp.dot(normed_two, w_gate.T, precision=highest))
    lifted = low_back(jnp.dot(normed_two, w_up.T, precision=highest))
    hidden = lower_precision(jax.nn.silu(gates) * lifted)
    unit_out = low_back(jnp.dot(hidden, w_down, precision=highest))
    return middle + unit_out

def reference(tokens, positions, gain_one, w_query, key_weight, value_weight, w_out, gain_two, w_gate, w_up, w_down, cotangent):
    weights = (gain_one.astype(jnp.float32), w_query.astype(jnp.float32), key_weight.astype(jnp.float32), value_weight.astype(jnp.float32), w_out.astype(jnp.float32), gain_two.astype(jnp.float32), w_gate.astype(jnp.float32), w_up.astype(jnp.float32), w_down.astype(jnp.float32))

    def one_sequence(carried, element):
        inputs, incoming, slot_positions = element

        def forward(values_in, *params):
            return layer(values_in, *params, slot_positions)
        result, pull = jax.vjp(forward, inputs.astype(jnp.float32), *weights)
        grads = pull(incoming.astype(jnp.float32))
        summed = tuple((grand_total + piece for grand_total, piece in zip(carried, grads[1:])))
        return (summed, (result.astype(jnp.bfloat16), grads[0].astype(jnp.bfloat16)))
    initial = tuple((jnp.zeros(weight.shape, jnp.float32) for weight in weights))
    sums, (outputs, grad_inputs) = lax.scan(one_sequence, initial, (tokens, cotangent, positions))
    return (outputs, grad_inputs, sums[0], sums[1], sums[2], sums[3], sums[4], sums[5], sums[6], sums[7], sums[8])
```

```python
import functools
import itertools

import jax
import jax.numpy as jnp
from jax import lax
from jax.experimental import pallas as pl
from jax.experimental.pallas import tpu as pltpu
from jax.sharding import PartitionSpec as P

QUERY_HEAD_COUNT = 15
KEY_VALUE_HEADS = 5
HEAD_WIDTH = 64
GROUP = QUERY_HEAD_COUNT // KEY_VALUE_HEADS
SLOT_ORDER = ("shard", "hi", "lo", "tensor")
VMEM_LIMIT = 50 * 1024 * 1024

epsilon = 1e-05


class Grid:
    def __init__(self, mesh):
        context = mesh.shape["context"]
        hi = 4 if context % 4 == 0 else 1
        self.size = {
            "shard": mesh.shape["shard"],
            "hi": hi,
            "lo": context // hi,
            "tensor": mesh.shape["tensor"],
        }

    def here(self):
        context = lax.axis_index("context")
        return {
            "shard": lax.axis_index("shard"),
            "hi": context // self.size["lo"],
            "lo": context % self.size["lo"],
            "tensor": lax.axis_index("tensor"),
        }

    def peer(self, me, axis, offset):
        there = (me[axis] + offset) % self.size[axis]
        if axis == "hi":
            return {"context": there * self.size["lo"] + me["lo"]}
        if axis == "lo":
            return {"context": me["hi"] * self.size["lo"] + there}
        return {axis: there}

    def slot(self, me, stages, offsets):
        place = dict(zip(stages, offsets))
        index = 0
        for axis in SLOT_ORDER:
            if axis in place:
                there = (me[axis] + place[axis]) % self.size[axis] if place[axis] else me[axis]
                index = index * self.size[axis] + there
        return index

    def count(self, stages):
        total = 1
        for axis in stages:
            total *= self.size[axis]
        return total


def greet(grid, me, axes):
    barrier = pltpu.get_barrier_semaphore()
    total = 0
    for axis in axes:
        for offset in range(1, grid.size[axis]):
            pl.semaphore_signal(
                barrier,
                inc=1,
                device_id=grid.peer(me, axis, offset),
                device_id_type=pl.DeviceIdType.MESH,
            )
            total += 1
    pl.semaphore_wait(barrier, total)


def remote(source, target, send, receive, device):
    return pltpu.make_async_remote_copy(
        src_ref=source,
        dst_ref=target,
        send_sem=send,
        recv_sem=receive,
        device_id=device,
        device_id_type=pl.DeviceIdType.MESH,
    )


def arrival(offsets):
    return max([at for at, offset in enumerate(offsets) if offset], default=-1)


def gather_sends(grid, stages):
    total = 0
    for offsets in itertools.product(*[range(grid.size[axis]) for axis in stages]):
        for axis in stages[arrival(offsets) + 1 :]:
            total += grid.size[axis] - 1
    return total


def flat_index(sizes, offsets):
    index = 0
    for size, offset in zip(sizes, offsets):
        index = index * size + offset
    return index


def gather_kernel(grid, plans, *refs):
    number = len(plans)
    sources, targets = refs[:number], refs[number : 2 * number]
    sems = refs[2 * number :]
    me = grid.here()
    greet(grid, me, [axis for axis in SLOT_ORDER if any(axis in stages for stages in plans)])
    sent = []

    def forward(at, stages, offsets, source, used):
        target, (send, receive, unused) = targets[at], sems[3 * at : 3 * at + 3]
        sizes = [grid.size[axis] for axis in stages]
        slot = grid.slot(me, stages, offsets)
        for stage in range(arrival(offsets) + 1, len(stages)):
            for step in range(1, sizes[stage]):
                landing = list(offsets)
                landing[stage] = (-step) % sizes[stage]
                copy = remote(
                    source,
                    target.at[slot],
                    send.at[used],
                    receive.at[flat_index(sizes, landing)],
                    grid.peer(me, stages[stage], step),
                )
                copy.start()
                sent.append(copy)
                used += 1
        return used

    used = [0] * number
    own = []
    for at, stages in enumerate(plans):
        none = (0,) * len(stages)
        used[at] = forward(at, stages, none, sources[at], used[at])
        copy = pltpu.make_async_copy(
            sources[at], targets[at].at[grid.slot(me, stages, none)], sems[3 * at + 2]
        )
        copy.start()
        own.append(copy)
    for at, stages in enumerate(plans):
        sizes = [grid.size[axis] for axis in stages]
        order = sorted(
            itertools.product(*[range(size) for size in sizes]),
            key=lambda offsets: (arrival(offsets), offsets),
        )
        for offsets in order:
            if arrival(offsets) < 0:
                continue
            block = targets[at].at[grid.slot(me, stages, offsets)]
            last = arrival(offsets)
            remote(
                block,
                block,
                sems[3 * at].at[0],
                sems[3 * at + 1].at[flat_index(sizes, offsets)],
                grid.peer(me, stages[last], offsets[last]),
            ).wait_recv()
            used[at] = forward(at, stages, offsets, block, used[at])
    for copy in sent:
        copy.wait_send()
    for copy in own:
        copy.wait()


def gather_blocks(grid, identity, arrays, plans):
    scratch = []
    for stages in plans:
        scratch += [
            pltpu.SemaphoreType.DMA((gather_sends(grid, stages),)),
            pltpu.SemaphoreType.DMA((grid.count(stages),)),
            pltpu.SemaphoreType.DMA,
        ]
    bytes_moved = sum(
        2 * grid.count(stages) * array.size * array.dtype.itemsize
        for array, stages in zip(arrays, plans)
    )
    return pl.pallas_call(
        functools.partial(gather_kernel, grid, plans),
        out_shape=[
            jax.ShapeDtypeStruct((grid.count(stages), *array.shape), array.dtype)
            for array, stages in zip(arrays, plans)
        ],
        in_specs=[pl.BlockSpec(memory_space=pl.ANY)] * len(plans),
        out_specs=[pl.BlockSpec(memory_space=pl.ANY)] * len(plans),
        scratch_shapes=scratch,
        compiler_params=pltpu.CompilerParams(collective_id=identity, has_side_effects=True),
        cost_estimate=pl.CostEstimate(
            flops=0, bytes_accessed=bytes_moved * 8, transcendentals=0
        ),
        name=f"gather_blocks_{identity}",
    )(*arrays)


def rest_count(grid, stages, stage):
    return (grid.size[stages[stage]] - 1) * grid.count(stages[stage + 1 :])


def rest_index(grid, stages, stage, offsets):
    index = offsets[stage] - 1
    for at in range(stage + 1, len(stages)):
        index = index * grid.size[stages[at]] + offsets[at]
    return index


def scatter_kernel(grid, plans, with_gains, *refs):
    number = len(plans)
    extra = 1 if with_gains else 0
    sources = refs[: number + extra]
    targets = refs[number + extra : 2 * (number + extra)]
    scratch = list(refs[2 * (number + extra) :])
    me = grid.here()
    greet(
        grid,
        me,
        [
            axis
            for axis in SLOT_ORDER
            if with_gains or any(axis in stages for stages in plans)
        ],
    )
    sent = []
    tasks = []
    for stages in plans:
        landing, leaving, send, receive = [], [None], [], []
        for stage in range(len(stages)):
            landing.append(scratch.pop(0))
            if stage:
                leaving.append(scratch.pop(0))
            send.append(scratch.pop(0))
            receive.append(scratch.pop(0))
        tasks.append((landing, leaving, send, receive))

    def pick(at, stages, stage):
        choices = [[0]] * stage + [range(1, grid.size[stages[stage]])]
        for axis in stages[stage + 1 :]:
            choices.append([*range(1, grid.size[axis]), 0])
        later = list(itertools.product(*choices))
        return sorted(later, key=lambda offsets: [offset == 0 for offset in reversed(offsets)])

    def push(at, stages, stage, offsets, source):
        landing, leaving, send, receive = tasks[at]
        index = rest_index(grid, stages, stage, offsets)
        copy = remote(
            source,
            landing[stage].at[index],
            send[stage].at[index],
            receive[stage].at[index],
            grid.peer(me, stages[stage], offsets[stage]),
        )
        copy.start()
        sent.append(copy)

    def total(at, stages, stage, offsets):
        landing, leaving, send, receive = tasks[at]
        parts = []
        for before in range(stage):
            for step in range(1, grid.size[stages[before]]):
                place = list(offsets)
                place[before] = step
                index = rest_index(grid, stages, before, place)
                block = landing[before].at[index]
                remote(
                    block,
                    block,
                    send[before].at[index],
                    receive[before].at[index],
                    grid.peer(me, stages[before], step),
                ).wait_recv()
                parts.append(block)
        amount = sources[at][grid.slot(me, stages, offsets)].astype(jnp.float32)
        for block in parts:
            amount = amount + block[...].astype(jnp.float32)
        return amount

    for at, stages in enumerate(plans):
        for offsets in pick(at, stages, 0):
            push(at, stages, 0, offsets, sources[at].at[grid.slot(me, stages, offsets)])
    if with_gains:
        amount = sources[number][...]
        for axis in ("tensor", "shard", "lo", "hi"):
            held, send, receive = scratch.pop(0), scratch.pop(0), scratch.pop(0)
            held[me[axis]] = amount
            copies = []
            for step in range(1, grid.size[axis]):
                copy = remote(
                    held.at[me[axis]],
                    held.at[me[axis]],
                    send.at[step - 1],
                    receive.at[step - 1],
                    grid.peer(me, axis, step),
                )
                copy.start()
                copies.append(copy)
            for step in range(1, grid.size[axis]):
                block = held.at[(me[axis] - step) % grid.size[axis]]
                remote(
                    block,
                    block,
                    send.at[step - 1],
                    receive.at[step - 1],
                    grid.peer(me, axis, step),
                ).wait_recv()
            amount = held[0]
            for index in range(1, grid.size[axis]):
                amount = amount + held[index]
            sent += copies
        targets[number][...] = amount
    for at, stages in enumerate(plans):
        for stage in range(1, len(stages)):
            for offsets in pick(at, stages, stage):
                leaving = tasks[at][1][stage].at[rest_index(grid, stages, stage, offsets)]
                leaving[...] = total(at, stages, stage, offsets).astype(leaving.dtype)
                push(at, stages, stage, offsets, leaving)
        targets[at][...] = total(at, stages, len(stages), (0,) * len(stages))
    for copy in sent:
        copy.wait_send()


def scatter_sums(grid, identity, arrays, plans, gains=None):
    scratch = []
    for array, stages in zip(arrays, plans):
        for stage in range(len(stages)):
            count = rest_count(grid, stages, stage)
            scratch.append(pltpu.VMEM((count, *array.shape[1:]), array.dtype))
            if stage:
                scratch.append(pltpu.VMEM((count, *array.shape[1:]), array.dtype))
            scratch += [pltpu.SemaphoreType.DMA((count,)), pltpu.SemaphoreType.DMA((count,))]
    outs = [jax.ShapeDtypeStruct(array.shape[1:], jnp.float32) for array in arrays]
    operands = list(arrays)
    if gains is not None:
        for axis in ("tensor", "shard", "lo", "hi"):
            size = grid.size[axis]
            scratch += [
                pltpu.VMEM((size, *gains.shape), gains.dtype),
                pltpu.SemaphoreType.DMA((max(size - 1, 1),)),
                pltpu.SemaphoreType.DMA((max(size - 1, 1),)),
            ]
        operands.append(gains)
        outs.append(jax.ShapeDtypeStruct(gains.shape, gains.dtype))
    bytes_moved = sum(2 * array.size * array.dtype.itemsize for array in arrays)
    return pl.pallas_call(
        functools.partial(scatter_kernel, grid, plans, gains is not None),
        out_shape=outs,
        in_specs=[pl.BlockSpec(memory_space=pltpu.VMEM)] * len(operands),
        out_specs=[pl.BlockSpec(memory_space=pltpu.VMEM)] * len(operands),
        scratch_shapes=scratch,
        compiler_params=pltpu.CompilerParams(
            collective_id=identity, has_side_effects=True, vmem_limit_bytes=VMEM_LIMIT
        ),
        cost_estimate=pl.CostEstimate(
            flops=0, bytes_accessed=bytes_moved * 8, transcendentals=0
        ),
        name=f"scatter_sums_{identity}",
    )(*operands)


def dot_last(left, right):
    return lax.dot_general(left, right, (((1,), (1,)), ((), ())), preferred_element_type=jnp.float32)


def dot_plain(left, right):
    return lax.dot_general(left, right, (((1,), (0,)), ((), ())), preferred_element_type=jnp.float32)


def attend_kernel(queries, keys, values, bias, mixed, norms):
    scores = dot_last(keys[0], queries[0]) + bias[...]
    highest = jnp.max(scores, axis=0, keepdims=True)
    weights = jnp.exp(scores - highest)
    sums = jnp.sum(weights, axis=0, keepdims=True)
    probs = (weights * (1.0 / sums)).astype(jnp.bfloat16)
    mixed[0] = dot_plain(values[0].T, probs).T.astype(mixed.dtype)
    norms[0] = highest + jnp.log(sums)


def attend_back_kernel(queries, keys, values, bias, norms, gradient, grad_q, grad_k, grad_v):
    scores = dot_last(keys[0], queries[0]) + bias[...]
    probs = jnp.exp(scores - norms[0])
    grad_probs = dot_last(values[0], gradient[0])
    delta = jnp.sum(probs * grad_probs, axis=0, keepdims=True)
    grad_scores = (probs * (grad_probs - delta)).astype(jnp.bfloat16)
    grad_q[0] = dot_plain(keys[0].T, grad_scores).T * HEAD_WIDTH ** (-0.5)
    grad_k[0] = dot_plain(grad_scores, queries[0]).astype(grad_k.dtype)
    grad_v[0] = dot_plain(probs.astype(jnp.bfloat16), gradient[0]).astype(grad_v.dtype)


def per_head(rows, columns):
    return pl.BlockSpec((1, rows, columns), lambda head: (head, 0, 0))


def attend(queries, keys, values, bias):
    total, rows = keys.shape[1], queries.shape[1]
    return pl.pallas_call(
        attend_kernel,
        grid=(KEY_VALUE_HEADS,),
        in_specs=[
            per_head(rows, HEAD_WIDTH),
            per_head(total, HEAD_WIDTH),
            per_head(total, HEAD_WIDTH),
            pl.BlockSpec((total, rows), lambda head: (0, 0)),
        ],
        out_specs=[per_head(rows, HEAD_WIDTH), per_head(1, rows)],
        out_shape=[
            jax.ShapeDtypeStruct((KEY_VALUE_HEADS, rows, HEAD_WIDTH), jnp.bfloat16),
            jax.ShapeDtypeStruct((KEY_VALUE_HEADS, 1, rows), jnp.float32),
        ],
        compiler_params=pltpu.CompilerParams(vmem_limit_bytes=VMEM_LIMIT),
        name="attend",
    )(queries, keys, values, bias)


def attend_back(queries, keys, values, bias, norms, gradient):
    total, rows = keys.shape[1], queries.shape[1]
    return pl.pallas_call(
        attend_back_kernel,
        grid=(KEY_VALUE_HEADS,),
        in_specs=[
            per_head(rows, HEAD_WIDTH),
            per_head(total, HEAD_WIDTH),
            per_head(total, HEAD_WIDTH),
            pl.BlockSpec((total, rows), lambda head: (0, 0)),
            per_head(1, rows),
            per_head(rows, HEAD_WIDTH),
        ],
        out_specs=[
            per_head(rows, HEAD_WIDTH),
            per_head(total, HEAD_WIDTH),
            per_head(total, HEAD_WIDTH),
        ],
        out_shape=[
            jax.ShapeDtypeStruct((KEY_VALUE_HEADS, rows, HEAD_WIDTH), jnp.float32),
            jax.ShapeDtypeStruct((KEY_VALUE_HEADS, total, HEAD_WIDTH), jnp.bfloat16),
            jax.ShapeDtypeStruct((KEY_VALUE_HEADS, total, HEAD_WIDTH), jnp.bfloat16),
        ],
        compiler_params=pltpu.CompilerParams(vmem_limit_bytes=VMEM_LIMIT),
        name="attend_back",
    )(queries, keys, values, bias, norms, gradient)


def rms_scale(value_matrix, gain):
    return (
        value_matrix
        * lax.rsqrt(jnp.mean(value_matrix * value_matrix, axis=-1, keepdims=True) + epsilon)
        * gain
    )


def apply_rotation(value_matrix, slot_positions, heads, direction):
    head_size = value_matrix.shape[1] // heads
    half_dim = head_size // 2
    freqs = 10000.0 ** (-jnp.arange(half_dim, dtype=jnp.float32) / half_dim)
    angles = slot_positions.astype(jnp.float32)[:, None] * freqs[None, :]
    cosine = jnp.cos(angles)[:, None, :]
    sine = direction * jnp.sin(angles)[:, None, :]
    split_heads = value_matrix.reshape(value_matrix.shape[0], heads, head_size)
    first_half = split_heads[..., :half_dim]
    second_half = split_heads[..., half_dim:]
    turned = jnp.concatenate(
        [first_half * cosine - second_half * sine, second_half * cosine + first_half * sine],
        axis=-1,
    )
    return turned.reshape(value_matrix.shape)


GATHER_PART = ("hi", "lo", "tensor")
GATHER_ALL = ("hi", "lo", "shard", "tensor")
SCATTER_PART = ("tensor", "lo", "hi")
SCATTER_ALL = ("tensor", "shard", "lo", "hi")


def to_groups(rows):
    count = rows.shape[0]
    split = rows.reshape(count, KEY_VALUE_HEADS, GROUP, HEAD_WIDTH)
    return split.transpose(1, 2, 0, 3).reshape(KEY_VALUE_HEADS, GROUP * count, HEAD_WIDTH)


def from_groups(groups):
    count = groups.shape[1] // GROUP
    split = groups.reshape(KEY_VALUE_HEADS, GROUP, count, HEAD_WIDTH)
    return split.transpose(2, 0, 1, 3).reshape(count, QUERY_HEAD_COUNT * HEAD_WIDTH)


def body(
    grid,
    tokens,
    positions,
    gain_one,
    w_query,
    key_weight,
    value_weight,
    w_out,
    gain_two,
    w_gate,
    w_up,
    w_down,
    cotangent,
):
    shards = grid.size["shard"]
    devices = grid.count(GATHER_PART)
    inputs = tokens[0].astype(jnp.float32)
    slot_positions = positions[0]
    incoming = cotangent[0].astype(jnp.float32)
    count = inputs.shape[0]
    width = inputs.shape[1]
    part = width // shards
    q_rows, k_rows, units = w_query.shape[0], key_weight.shape[0], w_gate.shape[0]
    kv_width = KEY_VALUE_HEADS * HEAD_WIDTH
    total_rows = devices * count

    cot_all = lax.all_gather(cotangent[0], ("context", "tensor"), axis=0, tiled=True)
    packed = jnp.concatenate([w_query, key_weight, value_weight, w_out], axis=0)
    (attention_blocks,) = gather_blocks(grid, 1, [packed], [GATHER_ALL])
    attention_w = attention_blocks.reshape(shards, devices, packed.shape[0], part)
    attention_w = attention_w.transpose(1, 2, 0, 3).reshape(devices, packed.shape[0], width)
    q_end, k_end, v_end = q_rows, q_rows + k_rows, q_rows + 2 * k_rows
    query_w = attention_w[:, :q_end].reshape(devices * q_rows, width)
    key_w = attention_w[:, q_end:k_end].reshape(devices * k_rows, width)
    value_w = attention_w[:, k_end:v_end].reshape(devices * k_rows, width)
    out_w = attention_w[:, v_end:].reshape(devices * q_rows, width)

    normed_one = rms_scale(inputs, gain_one).astype(jnp.bfloat16)
    queries = dot_last(normed_one, query_w)
    key_matrix = dot_last(normed_one, key_w)
    value_matrix = dot_last(normed_one, value_w).astype(jnp.bfloat16)
    rotated_queries = apply_rotation(queries, slot_positions, QUERY_HEAD_COUNT, 1.0).astype(
        jnp.bfloat16
    )
    rotated_keys = apply_rotation(key_matrix, slot_positions, KEY_VALUE_HEADS, 1.0).astype(
        jnp.bfloat16
    )
    block_number = (slot_positions[0] // count).astype(jnp.bfloat16)
    pack = jnp.concatenate([rotated_keys, value_matrix], axis=1)
    pack = jnp.concatenate([pack, jnp.broadcast_to(block_number, (16, 2 * kv_width))], axis=0)
    units_w = jnp.concatenate([w_gate, w_up, w_down], axis=0)
    gathered, units_blocks = gather_blocks(
        grid, 2, [pack, units_w], [GATHER_PART, ("shard",)]
    )
    block_numbers = gathered[:, count, 0].astype(jnp.int32)
    key_places = (block_numbers[:, None] * count + jnp.arange(count)[None, :]).reshape(total_rows)
    query_places = jnp.tile(slot_positions, GROUP)
    bias = jnp.where(key_places[:, None] <= query_places[None, :], 0.0, -1e30).astype(jnp.float32)
    by_head = gathered[:, :count].reshape(total_rows, 2, KEY_VALUE_HEADS, HEAD_WIDTH)
    by_head = by_head.transpose(1, 2, 0, 3)
    all_keys, all_values = by_head[0], by_head[1]
    grouped_queries = to_groups(rotated_queries) * jnp.bfloat16(HEAD_WIDTH ** (-0.5))
    mixed, norms = attend(grouped_queries, all_keys, all_values, bias)
    mixed_low = from_groups(mixed)

    middle = inputs + dot_last(mixed_low, out_w)
    normed_two = rms_scale(middle, gain_two).astype(jnp.bfloat16)
    (normed_blocks,) = gather_blocks(grid, 3, [normed_two], [GATHER_PART])
    normed_all = normed_blocks.reshape(total_rows, width)
    units_full = units_blocks.transpose(1, 0, 2).reshape(3 * units, width)
    gate_up = units_full[: 2 * units]
    down_w = units_full[2 * units :]
    gates_lifted = dot_last(normed_all, gate_up)
    gates, lifted = gates_lifted[:, :units], gates_lifted[:, units:]
    grad_hidden = dot_last(cot_all, down_w)
    sigmoid = jax.nn.sigmoid(gates)
    silu = gates * sigmoid
    hidden = (silu * lifted).astype(jnp.bfloat16)
    grad_gates = (grad_hidden * lifted * sigmoid * (1.0 + gates * (1.0 - sigmoid))).astype(
        jnp.bfloat16
    )
    grad_lifted = (grad_hidden * silu).astype(jnp.bfloat16)
    grad_both = jnp.concatenate([grad_gates, grad_lifted], axis=1)
    grad_norm_part = dot_plain(grad_both, gate_up).astype(jnp.bfloat16)
    unit_part = dot_plain(hidden, down_w).astype(jnp.bfloat16)
    (grad_normed_two,) = scatter_sums(
        grid, 4, [grad_norm_part.reshape(devices, count, width)], [SCATTER_PART]
    )
    unit_out = lax.psum_scatter(
        unit_part, ("context", "tensor"), scatter_dimension=0, tiled=True
    ).astype(jnp.float32)
    output = (middle + unit_out).astype(jnp.bfloat16)[None]

    unused_two, pull_two = jax.vjp(rms_scale, middle, gain_two)
    grad_middle_norm, grad_gain_two = pull_two(grad_normed_two)
    grad_middle = incoming + grad_middle_norm
    grad_branch = grad_middle.astype(jnp.bfloat16)
    mixed_gradient = dot_plain(grad_branch, out_w).astype(jnp.bfloat16)
    query_gradient, grad_keys, grad_values = attend_back(
        grouped_queries, all_keys, all_values, bias, norms, to_groups(mixed_gradient)
    )
    key_terms = jnp.stack([grad_keys, grad_values]).transpose(2, 0, 1, 3)
    key_terms = key_terms.reshape(devices, count, 2 * kv_width)
    grad_gate_up = jnp.dot(grad_both.T, normed_all, preferred_element_type=jnp.float32)
    grad_down = jnp.dot(hidden.T, cot_all, preferred_element_type=jnp.float32)
    grad_units = jnp.concatenate([grad_gate_up, grad_down], axis=0).astype(jnp.bfloat16)
    grad_units = grad_units.reshape(3 * units, shards, part).transpose(1, 0, 2)
    summed, unit_sums = scatter_sums(
        grid, 5, [key_terms, grad_units], [SCATTER_PART, ("shard",)]
    )
    grad_q = apply_rotation(
        from_groups(query_gradient), slot_positions, QUERY_HEAD_COUNT, -1.0
    ).astype(jnp.bfloat16)
    key_gradient = apply_rotation(
        summed[:, :kv_width], slot_positions, KEY_VALUE_HEADS, -1.0
    ).astype(jnp.bfloat16)
    grad_v = summed[:, kv_width:].astype(jnp.bfloat16)
    grad_normed_one = (
        dot_plain(grad_q, query_w) + dot_plain(key_gradient, key_w) + dot_plain(grad_v, value_w)
    )
    unused_one, pull_one = jax.vjp(rms_scale, inputs, gain_one)
    grad_inputs_norm, grad_gain_one = pull_one(grad_normed_one)
    grad_tokens = (grad_middle + grad_inputs_norm).astype(jnp.bfloat16)[None]

    def by_device(left, right):
        grad = jnp.dot(left.T, right, preferred_element_type=jnp.float32).astype(jnp.bfloat16)
        return grad.reshape(devices, grad.shape[0] // devices, shards, part)

    grads = jnp.concatenate(
        [
            by_device(grad_q, normed_one),
            by_device(key_gradient, normed_one),
            by_device(grad_v, normed_one),
            by_device(grad_branch, mixed_low),
        ],
        axis=1,
    )
    grads = grads.transpose(2, 0, 1, 3).reshape(shards * devices, packed.shape[0], part)
    gains = jnp.zeros((8, width), jnp.float32).at[0].set(grad_gain_one).at[1].set(grad_gain_two)
    sums, gain_sums = scatter_sums(grid, 6, [grads], [SCATTER_ALL], gains)
    return (
        output,
        grad_tokens,
        gain_sums[0],
        sums[:q_end],
        sums[q_end:k_end],
        sums[k_end:v_end],
        sums[v_end:],
        gain_sums[1],
        unit_sums[:units],
        unit_sums[units : 2 * units],
        unit_sums[2 * units :],
    )


def solution(mesh):
    placed = (
        P("shard", ("context", "tensor"), None),
        P("shard", ("context", "tensor")),
        P(),
        P(("context", "tensor"), "shard"),
        P(("context", "tensor"), "shard"),
        P(("context", "tensor"), "shard"),
        P(("context", "tensor"), "shard"),
        P(),
        P(("context", "tensor"), "shard"),
        P(("context", "tensor"), "shard"),
        P(("context", "tensor"), "shard"),
        P("shard", ("context", "tensor"), None),
    )
    return jax.shard_map(
        functools.partial(body, Grid(mesh)),
        mesh=mesh,
        in_specs=placed,
        out_specs=(
            P("shard", ("context", "tensor"), None),
            P("shard", ("context", "tensor"), None),
            P(),
            P(("context", "tensor"), "shard"),
            P(("context", "tensor"), "shard"),
            P(("context", "tensor"), "shard"),
            P(("context", "tensor"), "shard"),
            P(),
            P(("context", "tensor"), "shard"),
            P(("context", "tensor"), "shard"),
            P(("context", "tensor"), "shard"),
        ),
        check_vma=False,
    )
```

```python
import functools
import itertools

import jax
import jax.numpy as jnp
from jax import lax
from jax.experimental import pallas as pl
from jax.experimental.pallas import tpu as pltpu
from jax.sharding import PartitionSpec as P

QUERY_HEAD_COUNT = 15
KEY_VALUE_HEADS = 5
HEAD_WIDTH = 64
GROUP = QUERY_HEAD_COUNT // KEY_VALUE_HEADS
SLOT_ORDER = ("shard", "hi", "lo", "tensor")
VMEM_LIMIT = 50 * 1024 * 1024

epsilon = 1e-05


class Grid:
    def __init__(self, mesh):
        context = mesh.shape["context"]
        hi = 4 if context % 4 == 0 else 1
        self.size = {
            "shard": mesh.shape["shard"],
            "hi": hi,
            "lo": context // hi,
            "tensor": mesh.shape["tensor"],
        }

    def here(self):
        context = lax.axis_index("context")
        return {
            "shard": lax.axis_index("shard"),
            "hi": context // self.size["lo"],
            "lo": context % self.size["lo"],
            "tensor": lax.axis_index("tensor"),
        }

    def peer(self, me, axis, offset):
        there = (me[axis] + offset) % self.size[axis]
        if axis == "hi":
            return {"context": there * self.size["lo"] + me["lo"]}
        if axis == "lo":
            return {"context": me["hi"] * self.size["lo"] + there}
        return {axis: there}

    def slot(self, me, stages, offsets):
        place = dict(zip(stages, offsets))
        index = 0
        for axis in SLOT_ORDER:
            if axis in place:
                there = (me[axis] + place[axis]) % self.size[axis] if place[axis] else me[axis]
                index = index * self.size[axis] + there
        return index

    def count(self, stages):
        total = 1
        for axis in stages:
            total *= self.size[axis]
        return total


def greet(grid, me, axes):
    barrier = pltpu.get_barrier_semaphore()
    total = 0
    for axis in axes:
        for offset in range(1, grid.size[axis]):
            pl.semaphore_signal(
                barrier,
                inc=1,
                device_id=grid.peer(me, axis, offset),
                device_id_type=pl.DeviceIdType.MESH,
            )
            total += 1
    pl.semaphore_wait(barrier, total)


def remote(source, target, send, receive, device):
    return pltpu.make_async_remote_copy(
        src_ref=source,
        dst_ref=target,
        send_sem=send,
        recv_sem=receive,
        device_id=device,
        device_id_type=pl.DeviceIdType.MESH,
    )


def arrival(offsets):
    return max([at for at, offset in enumerate(offsets) if offset], default=-1)


def gather_sends(grid, stages):
    total = 0
    for offsets in itertools.product(*[range(grid.size[axis]) for axis in stages]):
        for axis in stages[arrival(offsets) + 1 :]:
            total += grid.size[axis] - 1
    return total


def flat_index(sizes, offsets):
    index = 0
    for size, offset in zip(sizes, offsets):
        index = index * size + offset
    return index


def gather_kernel(grid, plans, *refs):
    number = len(plans)
    sources, targets = refs[:number], refs[number : 2 * number]
    sems = refs[2 * number :]
    me = grid.here()
    greet(grid, me, [axis for axis in SLOT_ORDER if any(axis in stages for stages in plans)])
    sent = []

    def forward(at, stages, offsets, source, used):
        target, (send, receive, unused) = targets[at], sems[3 * at : 3 * at + 3]
        sizes = [grid.size[axis] for axis in stages]
        slot = grid.slot(me, stages, offsets)
        for stage in range(arrival(offsets) + 1, len(stages)):
            for step in range(1, sizes[stage]):
                landing = list(offsets)
                landing[stage] = (-step) % sizes[stage]
                copy = remote(
                    source,
                    target.at[slot],
                    send.at[used],
                    receive.at[flat_index(sizes, landing)],
                    grid.peer(me, stages[stage], step),
                )
                copy.start()
                sent.append(copy)
                used += 1
        return used

    used = [0] * number
    own = []
    for at, stages in enumerate(plans):
        none = (0,) * len(stages)
        used[at] = forward(at, stages, none, sources[at], used[at])
        copy = pltpu.make_async_copy(
            sources[at], targets[at].at[grid.slot(me, stages, none)], sems[3 * at + 2]
        )
        copy.start()
        own.append(copy)
    for stage in range(max(len(stages) for stages in plans)):
        everything = []
        for at, stages in enumerate(plans):
            choices = itertools.product(*[range(grid.size[axis]) for axis in stages])
            listed = [offsets for offsets in choices if arrival(offsets) == stage]
            everything += [(turn, at, offsets) for turn, offsets in enumerate(listed)]
        for turn, at, offsets in sorted(everything):
            stages = plans[at]
            sizes = [grid.size[axis] for axis in stages]
            block = targets[at].at[grid.slot(me, stages, offsets)]
            last = arrival(offsets)
            remote(
                block,
                block,
                sems[3 * at].at[0],
                sems[3 * at + 1].at[flat_index(sizes, offsets)],
                grid.peer(me, stages[last], offsets[last]),
            ).wait_recv()
            used[at] = forward(at, stages, offsets, block, used[at])
    for copy in sent:
        copy.wait_send()
    for copy in own:
        copy.wait()


def gather_blocks(grid, identity, arrays, plans):
    scratch = []
    for stages in plans:
        scratch += [
            pltpu.SemaphoreType.DMA((gather_sends(grid, stages),)),
            pltpu.SemaphoreType.DMA((grid.count(stages),)),
            pltpu.SemaphoreType.DMA,
        ]
    bytes_moved = sum(
        2 * grid.count(stages) * array.size * array.dtype.itemsize
        for array, stages in zip(arrays, plans)
    )
    return pl.pallas_call(
        functools.partial(gather_kernel, grid, plans),
        out_shape=[
            jax.ShapeDtypeStruct((grid.count(stages), *array.shape), array.dtype)
            for array, stages in zip(arrays, plans)
        ],
        in_specs=[pl.BlockSpec(memory_space=pl.ANY)] * len(plans),
        out_specs=[pl.BlockSpec(memory_space=pl.ANY)] * len(plans),
        scratch_shapes=scratch,
        compiler_params=pltpu.CompilerParams(collective_id=identity, has_side_effects=True),
        cost_estimate=pl.CostEstimate(
            flops=0, bytes_accessed=bytes_moved * 8, transcendentals=0
        ),
        name=f"gather_blocks_{identity}",
    )(*arrays)


def rest_count(grid, stages, stage):
    return (grid.size[stages[stage]] - 1) * grid.count(stages[stage + 1 :])


def rest_index(grid, stages, stage, offsets):
    index = offsets[stage] - 1
    for at in range(stage + 1, len(stages)):
        index = index * grid.size[stages[at]] + offsets[at]
    return index


def scatter_kernel(grid, plans, with_gains, *refs):
    number = len(plans)
    extra = 1 if with_gains else 0
    sources = refs[: number + extra]
    targets = refs[number + extra : 2 * (number + extra)]
    scratch = list(refs[2 * (number + extra) :])
    me = grid.here()
    greet(
        grid,
        me,
        [
            axis
            for axis in SLOT_ORDER
            if with_gains or any(axis in stages for stages in plans)
        ],
    )
    sent = []
    tasks = []
    for stages in plans:
        landing, leaving, send, receive = [], [None], [], []
        for stage in range(len(stages)):
            landing.append(scratch.pop(0))
            if stage:
                leaving.append(scratch.pop(0))
            send.append(scratch.pop(0))
            receive.append(scratch.pop(0))
        tasks.append((landing, leaving, send, receive))

    def pick(at, stages, stage):
        choices = [[0]] * stage + [range(1, grid.size[stages[stage]])]
        for axis in stages[stage + 1 :]:
            choices.append([*range(1, grid.size[axis]), 0])
        later = list(itertools.product(*choices))
        return sorted(later, key=lambda offsets: [offset == 0 for offset in reversed(offsets)])

    def push(at, stages, stage, offsets, source):
        landing, leaving, send, receive = tasks[at]
        index = rest_index(grid, stages, stage, offsets)
        copy = remote(
            source,
            landing[stage].at[index],
            send[stage].at[index],
            receive[stage].at[index],
            grid.peer(me, stages[stage], offsets[stage]),
        )
        copy.start()
        sent.append(copy)

    def total(at, stages, stage, offsets):
        landing, leaving, send, receive = tasks[at]
        parts = []
        for before in range(stage):
            for step in range(1, grid.size[stages[before]]):
                place = list(offsets)
                place[before] = step
                index = rest_index(grid, stages, before, place)
                block = landing[before].at[index]
                remote(
                    block,
                    block,
                    send[before].at[index],
                    receive[before].at[index],
                    grid.peer(me, stages[before], step),
                ).wait_recv()
                parts.append(block)
        amount = sources[at][grid.slot(me, stages, offsets)].astype(jnp.float32)
        for block in parts:
            amount = amount + block[...].astype(jnp.float32)
        return amount

    for at, stages in enumerate(plans):
        for offsets in pick(at, stages, 0):
            push(at, stages, 0, offsets, sources[at].at[grid.slot(me, stages, offsets)])
    if with_gains:
        amount = sources[number][...]
        for axis in ("tensor", "shard", "lo", "hi"):
            held, send, receive = scratch.pop(0), scratch.pop(0), scratch.pop(0)
            held[me[axis]] = amount
            copies = []
            for step in range(1, grid.size[axis]):
                copy = remote(
                    held.at[me[axis]],
                    held.at[me[axis]],
                    send.at[step - 1],
                    receive.at[step - 1],
                    grid.peer(me, axis, step),
                )
                copy.start()
                copies.append(copy)
            for step in range(1, grid.size[axis]):
                block = held.at[(me[axis] - step) % grid.size[axis]]
                remote(
                    block,
                    block,
                    send.at[step - 1],
                    receive.at[step - 1],
                    grid.peer(me, axis, step),
                ).wait_recv()
            amount = held[0]
            for index in range(1, grid.size[axis]):
                amount = amount + held[index]
            sent += copies
        targets[number][...] = amount
    for stage in range(1, max(len(stages) for stages in plans)):
        everything = []
        for at, stages in enumerate(plans):
            if stage < len(stages):
                everything += [
                    (turn, at, offsets)
                    for turn, offsets in enumerate(pick(at, stages, stage))
                ]
        if everything:
            for turn, at, offsets in sorted(everything):
                stages = plans[at]
                leaving = tasks[at][1][stage].at[rest_index(grid, stages, stage, offsets)]
                leaving[...] = total(at, stages, stage, offsets).astype(leaving.dtype)
                push(at, stages, stage, offsets, leaving)
    for at, stages in enumerate(plans):
        targets[at][...] = total(at, stages, len(stages), (0,) * len(stages))
    for copy in sent:
        copy.wait_send()


def scatter_sums(grid, identity, arrays, plans, gains=None):
    scratch = []
    for array, stages in zip(arrays, plans):
        for stage in range(len(stages)):
            count = rest_count(grid, stages, stage)
            scratch.append(pltpu.VMEM((count, *array.shape[1:]), array.dtype))
            if stage:
                scratch.append(pltpu.VMEM((count, *array.shape[1:]), array.dtype))
            scratch += [pltpu.SemaphoreType.DMA((count,)), pltpu.SemaphoreType.DMA((count,))]
    outs = [jax.ShapeDtypeStruct(array.shape[1:], jnp.float32) for array in arrays]
    operands = list(arrays)
    if gains is not None:
        for axis in ("tensor", "shard", "lo", "hi"):
            size = grid.size[axis]
            scratch += [
                pltpu.VMEM((size, *gains.shape), gains.dtype),
                pltpu.SemaphoreType.DMA((max(size - 1, 1),)),
                pltpu.SemaphoreType.DMA((max(size - 1, 1),)),
            ]
        operands.append(gains)
        outs.append(jax.ShapeDtypeStruct(gains.shape, gains.dtype))
    bytes_moved = sum(2 * array.size * array.dtype.itemsize for array in arrays)
    return pl.pallas_call(
        functools.partial(scatter_kernel, grid, plans, gains is not None),
        out_shape=outs,
        in_specs=[pl.BlockSpec(memory_space=pltpu.VMEM)] * len(operands),
        out_specs=[pl.BlockSpec(memory_space=pltpu.VMEM)] * len(operands),
        scratch_shapes=scratch,
        compiler_params=pltpu.CompilerParams(
            collective_id=identity, has_side_effects=True, vmem_limit_bytes=VMEM_LIMIT
        ),
        cost_estimate=pl.CostEstimate(
            flops=0, bytes_accessed=bytes_moved * 8, transcendentals=0
        ),
        name=f"scatter_sums_{identity}",
    )(*operands)


def dot_last(left, right):
    return lax.dot_general(left, right, (((1,), (1,)), ((), ())), preferred_element_type=jnp.float32)


def dot_plain(left, right):
    return lax.dot_general(left, right, (((1,), (0,)), ((), ())), preferred_element_type=jnp.float32)


def dot_first(left, right):
    return lax.dot_general(left, right, (((0,), (0,)), ((), ())), preferred_element_type=jnp.float32)


def side_by_side(ref):
    return jnp.concatenate([ref[index] for index in range(ref.shape[0])], axis=1)


def spread(ref, amount):
    width = ref.shape[2]
    for index in range(ref.shape[0]):
        ref[index] = amount[:, index * width : (index + 1) * width].astype(ref.dtype)


def attend_kernel(queries, keys, values, bias, mixed, norms):
    scores = dot_first(side_by_side(keys), side_by_side(queries)) + bias[...]
    highest = jnp.max(scores, axis=0, keepdims=True)
    weights = jnp.exp(scores - highest)
    sums = jnp.sum(weights, axis=0, keepdims=True)
    probs = (weights * (1.0 / sums)).astype(jnp.bfloat16)
    spread(mixed, dot_plain(side_by_side(values), probs))
    norms[0] = highest + jnp.log(sums)


def attend_back_kernel(queries, keys, values, bias, norms, gradient, grad_q, grad_k, grad_v):
    all_queries, all_keys = side_by_side(queries), side_by_side(keys)
    all_gradients = side_by_side(gradient)
    scores = dot_first(all_keys, all_queries) + bias[...]
    probs = jnp.exp(scores - norms[0])
    grad_probs = dot_first(side_by_side(values), all_gradients)
    delta = jnp.sum(probs * grad_probs, axis=0, keepdims=True)
    grad_scores = (probs * (grad_probs - delta)).astype(jnp.bfloat16)
    spread(grad_q, dot_plain(all_keys, grad_scores) * HEAD_WIDTH ** (-0.5))
    spread(grad_k, dot_last(all_queries, grad_scores))
    spread(grad_v, dot_last(all_gradients, probs.astype(jnp.bfloat16)))


def group_spec(count):
    return pl.BlockSpec((GROUP, HEAD_WIDTH, count), lambda head: (head, 0, 0))


def pair_spec(blocks, count, shift):
    return pl.BlockSpec((blocks, HEAD_WIDTH, count), lambda head: (0, head + shift, 0))


def row_spec(rows):
    return pl.BlockSpec((1, 1, rows), lambda head: (head, 0, 0))


def attend(queries, pairs, bias):
    blocks, unused, count = pairs.shape
    rows = GROUP * count
    return pl.pallas_call(
        attend_kernel,
        grid=(KEY_VALUE_HEADS,),
        in_specs=[
            group_spec(count),
            pair_spec(blocks, count, 0),
            pair_spec(blocks, count, KEY_VALUE_HEADS),
            pl.BlockSpec(bias.shape, lambda head: (0, 0)),
        ],
        out_specs=[group_spec(count), row_spec(rows)],
        out_shape=[
            jax.ShapeDtypeStruct(queries.shape, jnp.bfloat16),
            jax.ShapeDtypeStruct((KEY_VALUE_HEADS, 1, rows), jnp.float32),
        ],
        compiler_params=pltpu.CompilerParams(vmem_limit_bytes=VMEM_LIMIT),
        name="attend",
    )(queries, pairs, pairs, bias)


def attend_back(queries, pairs, bias, norms, gradient):
    blocks, unused, count = pairs.shape
    rows = GROUP * count
    grad_pair = jax.ShapeDtypeStruct((blocks, KEY_VALUE_HEADS * HEAD_WIDTH, count), jnp.bfloat16)
    return pl.pallas_call(
        attend_back_kernel,
        grid=(KEY_VALUE_HEADS,),
        in_specs=[
            group_spec(count),
            pair_spec(blocks, count, 0),
            pair_spec(blocks, count, KEY_VALUE_HEADS),
            pl.BlockSpec(bias.shape, lambda head: (0, 0)),
            row_spec(rows),
            group_spec(count),
        ],
        out_specs=[
            group_spec(count),
            pair_spec(blocks, count, 0),
            pair_spec(blocks, count, 0),
        ],
        out_shape=[jax.ShapeDtypeStruct(queries.shape, jnp.float32), grad_pair, grad_pair],
        compiler_params=pltpu.CompilerParams(vmem_limit_bytes=VMEM_LIMIT),
        name="attend_back",
    )(queries, pairs, pairs, bias, norms, gradient)


def units_kernel(units, normed, cot, weights, grad_norm, unit_out, grads):
    gate_w, up_w = weights[:units], weights[units : 2 * units]
    down_w = weights[2 * units :]
    rows, incoming = normed[...], cot[...]
    gates, lifted = dot_last(rows, gate_w), dot_last(rows, up_w)
    grad_hidden = dot_last(incoming, down_w)
    sigmoid = jax.nn.sigmoid(gates)
    silu = gates * sigmoid
    hidden = (silu * lifted).astype(jnp.bfloat16)
    grad_gates = (grad_hidden * lifted * sigmoid * (1.0 + gates * (1.0 - sigmoid))).astype(
        jnp.bfloat16
    )
    grad_lifted = (grad_hidden * silu).astype(jnp.bfloat16)
    grad_norm[...] = (dot_plain(grad_gates, gate_w) + dot_plain(grad_lifted, up_w)).astype(
        grad_norm.dtype
    )
    unit_out[...] = dot_plain(hidden, down_w).astype(unit_out.dtype)

    @pl.when(pl.program_id(0) == 0)
    def clear():
        grads[...] = jnp.zeros_like(grads)

    grads[:units] += dot_first(grad_gates, rows)
    grads[units : 2 * units] += dot_first(grad_lifted, rows)
    grads[2 * units :] += dot_first(hidden, incoming)


def feed_forward(normed, cot, weights):
    total, width = normed.shape
    rows = 256
    units = weights.shape[0] // 3
    by_rows = pl.BlockSpec((rows, width), lambda step: (step, 0))
    whole = pl.BlockSpec(weights.shape, lambda step: (0, 0))
    return pl.pallas_call(
        functools.partial(units_kernel, units),
        grid=(total // rows,),
        in_specs=[by_rows, by_rows, whole],
        out_specs=[by_rows, by_rows, whole],
        out_shape=[
            jax.ShapeDtypeStruct(normed.shape, jnp.bfloat16),
            jax.ShapeDtypeStruct(normed.shape, jnp.bfloat16),
            jax.ShapeDtypeStruct(weights.shape, jnp.float32),
        ],
        compiler_params=pltpu.CompilerParams(vmem_limit_bytes=VMEM_LIMIT),
        name="feed_forward",
    )(normed, cot, weights)


def rms_scale(value_matrix, gain):
    return (
        value_matrix
        * lax.rsqrt(jnp.mean(value_matrix * value_matrix, axis=-1, keepdims=True) + epsilon)
        * gain
    )


def apply_rotation(features, slot_positions, direction):
    half_dim = HEAD_WIDTH // 2
    freqs = 10000.0 ** (-jnp.arange(half_dim, dtype=jnp.float32) / half_dim)
    angles = freqs[:, None] * slot_positions.astype(jnp.float32)[None, :]
    cosine = jnp.cos(angles)[None]
    sine = direction * jnp.sin(angles)[None]
    heads = features.shape[0] // HEAD_WIDTH
    split_heads = features.reshape(heads, HEAD_WIDTH, features.shape[1])
    first_half = split_heads[:, :half_dim]
    second_half = split_heads[:, half_dim:]
    return jnp.concatenate(
        [first_half * cosine - second_half * sine, second_half * cosine + first_half * sine],
        axis=1,
    ).reshape(features.shape)


GATHER_PART = ("hi", "lo", "tensor")
GATHER_ALL = [("hi", "lo", "shard", "tensor"), ("hi", "shard", "lo", "tensor")]
SCATTER_PART = ("tensor", "lo", "hi")
SCATTER_ALL = [("tensor", "shard", "lo", "hi"), ("tensor", "lo", "shard", "hi")]


def body(
    grid,
    tokens,
    positions,
    gain_one,
    w_query,
    key_weight,
    value_weight,
    w_out,
    gain_two,
    w_gate,
    w_up,
    w_down,
    cotangent,
):
    shards = grid.size["shard"]
    devices = grid.count(GATHER_PART)
    inputs = tokens[0].astype(jnp.float32)
    slot_positions = positions[0]
    incoming = cotangent[0].astype(jnp.float32)
    count, width = inputs.shape
    part = width // shards
    q_rows, k_rows, units = w_query.shape[0], key_weight.shape[0], w_gate.shape[0]
    both = q_rows + k_rows
    kv_width = KEY_VALUE_HEADS * HEAD_WIDTH
    total_rows = devices * count
    flat = devices * both

    def columns(rows):
        return [rows[:, at * part : (at + 1) * part] for at in range(shards)]

    def sum_halves(weights, halves, dot):
        total = dot(weights[0], halves[0])
        for at in range(1, shards):
            total = total + dot(weights[at], halves[at])
        return total.reshape(devices, both, count)

    cot_all = lax.all_gather(cotangent[0], ("context", "tensor"), axis=0, tiled=True)
    first_blocks, second_blocks = gather_blocks(
        grid,
        1,
        [
            jnp.concatenate([w_query, key_weight], axis=0),
            jnp.concatenate([value_weight, w_out], axis=0),
        ],
        GATHER_ALL,
    )
    first_w = first_blocks.reshape(shards, flat, part)
    second_w = second_blocks.reshape(shards, flat, part)

    normed_one = rms_scale(inputs, gain_one).astype(jnp.bfloat16)
    normed_halves = columns(normed_one)
    first = sum_halves(first_w, normed_halves, dot_last)
    second = sum_halves(second_w, normed_halves, dot_last)
    queries = first[:, :q_rows].reshape(width, count)
    keys = first[:, q_rows:].reshape(kv_width, count)
    values = second[:, :k_rows].reshape(kv_width, count).astype(jnp.bfloat16)
    turned_q = apply_rotation(queries, slot_positions, 1.0).astype(jnp.bfloat16)
    turned_k = apply_rotation(keys, slot_positions, 1.0).astype(jnp.bfloat16)
    block_number = (slot_positions[0] // count).astype(jnp.bfloat16)
    pack = jnp.concatenate(
        [turned_k, values, jnp.broadcast_to(block_number, (16, count))], axis=0
    )
    units_w = jnp.concatenate([w_gate, w_up, w_down], axis=0)
    pairs, units_blocks = gather_blocks(grid, 2, [pack, units_w], [GATHER_PART, ("shard",)])
    block_numbers = pairs[:, 2 * kv_width, 0].astype(jnp.int32)
    key_places = (block_numbers[:, None] * count + jnp.arange(count)[None, :]).reshape(total_rows)
    query_places = jnp.tile(slot_positions, GROUP)
    bias = jnp.where(key_places[:, None] <= query_places[None, :], 0.0, -1e30).astype(jnp.float32)
    grouped_queries = (turned_q * jnp.bfloat16(HEAD_WIDTH ** (-0.5))).reshape(
        QUERY_HEAD_COUNT, HEAD_WIDTH, count
    )
    mixed, norms = attend(grouped_queries, pairs, bias)
    mixed_halves = mixed.reshape(shards, part, count)

    branch = sum_halves(second_w, mixed_halves, dot_plain)[:, k_rows:].reshape(width, count)
    middle = inputs + branch.T
    normed_two = rms_scale(middle, gain_two).astype(jnp.bfloat16)
    (normed_blocks,) = gather_blocks(grid, 3, [normed_two], [GATHER_PART])
    normed_all = normed_blocks.reshape(total_rows, width)
    units_full = units_blocks.transpose(1, 0, 2).reshape(3 * units, width)
    grad_norm_part, unit_part, grad_units = feed_forward(normed_all, cot_all, units_full)
    (grad_normed_two,) = scatter_sums(
        grid, 4, [grad_norm_part.reshape(devices, count, width)], [SCATTER_PART]
    )
    unit_part, grad_normed_two = lax.optimization_barrier((unit_part, grad_normed_two))
    unit_out = lax.psum_scatter(
        unit_part, ("context", "tensor"), scatter_dimension=0, tiled=True
    ).astype(jnp.float32)
    output = (middle + unit_out).astype(jnp.bfloat16)[None]

    unused_two, pull_two = jax.vjp(rms_scale, middle, gain_two)
    grad_middle_norm, grad_gain_two = pull_two(grad_normed_two)
    grad_middle = incoming + grad_middle_norm
    grad_branch = grad_middle.astype(jnp.bfloat16)
    blank_k = jnp.zeros((devices, k_rows, count), jnp.bfloat16)
    blank_q = jnp.zeros((devices, q_rows, count), jnp.bfloat16)
    grad_out_rows = jnp.concatenate(
        [blank_k, grad_branch.T.reshape(devices, q_rows, count)], axis=1
    ).reshape(flat, count)
    mixed_gradient = jnp.concatenate(
        [dot_first(second_w[at], grad_out_rows) for at in range(shards)], axis=0
    ).astype(jnp.bfloat16)
    query_gradient, grad_keys, grad_values = attend_back(
        grouped_queries, pairs, bias, norms, mixed_gradient.reshape(grouped_queries.shape)
    )
    grad_units = grad_units.astype(jnp.bfloat16).reshape(3 * units, shards, part)
    key_sum, value_sum, unit_sums = scatter_sums(
        grid,
        5,
        [grad_keys, grad_values, grad_units.transpose(1, 0, 2)],
        [SCATTER_PART, SCATTER_PART, ("shard",)],
    )
    grad_q = apply_rotation(query_gradient.reshape(width, count), slot_positions, -1.0)
    grad_k = apply_rotation(key_sum, slot_positions, -1.0)
    first_rows = jnp.concatenate(
        [
            grad_q.astype(jnp.bfloat16).reshape(devices, q_rows, count),
            grad_k.astype(jnp.bfloat16).reshape(devices, k_rows, count),
        ],
        axis=1,
    ).reshape(flat, count)
    value_rows = jnp.concatenate(
        [value_sum.astype(jnp.bfloat16).reshape(devices, k_rows, count), blank_q], axis=1
    ).reshape(flat, count)
    grad_normed_one = jnp.concatenate(
        [
            dot_first(first_rows, first_w[at]) + dot_first(value_rows, second_w[at])
            for at in range(shards)
        ],
        axis=1,
    )
    unused_one, pull_one = jax.vjp(rms_scale, inputs, gain_one)
    grad_inputs_norm, grad_gain_one = pull_one(grad_normed_one)
    grad_tokens = (grad_middle + grad_inputs_norm).astype(jnp.bfloat16)[None]
    first_grads = jnp.stack(
        [dot_plain(first_rows, half).astype(jnp.bfloat16) for half in normed_halves]
    )
    second_grads = jnp.stack(
        [
            (
                dot_plain(value_rows, normed_halves[at])
                + dot_last(grad_out_rows, mixed_halves[at])
            ).astype(jnp.bfloat16)
            for at in range(shards)
        ]
    )
    gains = jnp.zeros((8, width), jnp.float32).at[0].set(grad_gain_one).at[1].set(grad_gain_two)
    first_sums, second_sums, gain_sums = scatter_sums(
        grid,
        6,
        [
            first_grads.reshape(shards * devices, both, part),
            second_grads.reshape(shards * devices, both, part),
        ],
        SCATTER_ALL,
        gains,
    )
    return (
        output,
        grad_tokens,
        gain_sums[0],
        first_sums[:q_rows],
        first_sums[q_rows:],
        second_sums[:k_rows],
        second_sums[k_rows:],
        gain_sums[1],
        unit_sums[:units],
        unit_sums[units : 2 * units],
        unit_sums[2 * units :],
    )


def solution(mesh):
    placed = (
        P("shard", ("context", "tensor"), None),
        P("shard", ("context", "tensor")),
        P(),
        P(("context", "tensor"), "shard"),
        P(("context", "tensor"), "shard"),
        P(("context", "tensor"), "shard"),
        P(("context", "tensor"), "shard"),
        P(),
        P(("context", "tensor"), "shard"),
        P(("context", "tensor"), "shard"),
        P(("context", "tensor"), "shard"),
        P("shard", ("context", "tensor"), None),
    )
    return jax.shard_map(
        functools.partial(body, Grid(mesh)),
        mesh=mesh,
        in_specs=placed,
        out_specs=(
            P("shard", ("context", "tensor"), None),
            P("shard", ("context", "tensor"), None),
            P(),
            P(("context", "tensor"), "shard"),
            P(("context", "tensor"), "shard"),
            P(("context", "tensor"), "shard"),
            P(("context", "tensor"), "shard"),
            P(),
            P(("context", "tensor"), "shard"),
            P(("context", "tensor"), "shard"),
            P(("context", "tensor"), "shard"),
        ),
        check_vma=False,
    )
```

```python
import functools
import itertools

import jax
import jax.numpy as jnp
from jax import lax
from jax.experimental import pallas as pl
from jax.experimental.pallas import tpu as pltpu
from jax.sharding import PartitionSpec as P

QUERY_HEAD_COUNT = 15
KEY_VALUE_HEADS = 5
HEAD_WIDTH = 64
GROUP = QUERY_HEAD_COUNT // KEY_VALUE_HEADS
SLOT_ORDER = ("shard", "hi", "lo", "tensor")
VMEM_LIMIT = 50 * 1024 * 1024

epsilon = 1e-05


class Grid:
    def __init__(self, mesh):
        context = mesh.shape["context"]
        hi = 4 if context % 4 == 0 else 1
        self.size = {
            "shard": mesh.shape["shard"],
            "hi": hi,
            "lo": context // hi,
            "tensor": mesh.shape["tensor"],
        }

    def here(self):
        context = lax.axis_index("context")
        return {
            "shard": lax.axis_index("shard"),
            "hi": context // self.size["lo"],
            "lo": context % self.size["lo"],
            "tensor": lax.axis_index("tensor"),
        }

    def peer(self, me, axis, offset):
        there = (me[axis] + offset) % self.size[axis]
        if axis == "hi":
            return {"context": there * self.size["lo"] + me["lo"]}
        if axis == "lo":
            return {"context": me["hi"] * self.size["lo"] + there}
        return {axis: there}

    def slot(self, me, stages, offsets):
        place = dict(zip(stages, offsets))
        index = 0
        for axis in SLOT_ORDER:
            if axis in place:
                there = (me[axis] + place[axis]) % self.size[axis] if place[axis] else me[axis]
                index = index * self.size[axis] + there
        return index

    def count(self, stages):
        total = 1
        for axis in stages:
            total *= self.size[axis]
        return total


def greet(grid, me, axes):
    barrier = pltpu.get_barrier_semaphore()
    total = 0
    for axis in axes:
        for offset in range(1, grid.size[axis]):
            pl.semaphore_signal(
                barrier,
                inc=1,
                device_id=grid.peer(me, axis, offset),
                device_id_type=pl.DeviceIdType.MESH,
            )
            total += 1
    pl.semaphore_wait(barrier, total)


def remote(source, target, send, receive, device):
    return pltpu.make_async_remote_copy(
        src_ref=source,
        dst_ref=target,
        send_sem=send,
        recv_sem=receive,
        device_id=device,
        device_id_type=pl.DeviceIdType.MESH,
    )


def arrival(offsets):
    return max([at for at, offset in enumerate(offsets) if offset], default=-1)


def gather_sends(grid, stages):
    total = 0
    for offsets in itertools.product(*[range(grid.size[axis]) for axis in stages]):
        for axis in stages[arrival(offsets) + 1 :]:
            total += grid.size[axis] - 1
    return total


def flat_index(sizes, offsets):
    index = 0
    for size, offset in zip(sizes, offsets):
        index = index * size + offset
    return index


def gather_kernel(grid, plans, *refs):
    number = len(plans)
    sources, targets = refs[:number], refs[number : 2 * number]
    sems = refs[2 * number :]
    me = grid.here()
    greet(grid, me, [axis for axis in SLOT_ORDER if any(axis in stages for stages in plans)])
    sent = []

    def forward(at, stages, offsets, source, used):
        target, (send, receive, unused) = targets[at], sems[3 * at : 3 * at + 3]
        sizes = [grid.size[axis] for axis in stages]
        slot = grid.slot(me, stages, offsets)
        for stage in range(arrival(offsets) + 1, len(stages)):
            for step in range(1, sizes[stage]):
                landing = list(offsets)
                landing[stage] = (-step) % sizes[stage]
                copy = remote(
                    source,
                    target.at[slot],
                    send.at[used],
                    receive.at[flat_index(sizes, landing)],
                    grid.peer(me, stages[stage], step),
                )
                copy.start()
                sent.append(copy)
                used += 1
        return used

    used = [0] * number
    own = []
    for at, stages in enumerate(plans):
        none = (0,) * len(stages)
        used[at] = forward(at, stages, none, sources[at], used[at])
        copy = pltpu.make_async_copy(
            sources[at], targets[at].at[grid.slot(me, stages, none)], sems[3 * at + 2]
        )
        copy.start()
        own.append(copy)
    for stage in range(max(len(stages) for stages in plans)):
        everything = []
        for at, stages in enumerate(plans):
            choices = itertools.product(*[range(grid.size[axis]) for axis in stages])
            listed = [offsets for offsets in choices if arrival(offsets) == stage]
            everything += [(turn, at, offsets) for turn, offsets in enumerate(listed)]
        if number > 2:
            everything.sort(key=lambda item: (item[1], item[0]))
        else:
            everything.sort()
        for turn, at, offsets in everything:
            stages = plans[at]
            sizes = [grid.size[axis] for axis in stages]
            block = targets[at].at[grid.slot(me, stages, offsets)]
            last = arrival(offsets)
            remote(
                block,
                block,
                sems[3 * at].at[0],
                sems[3 * at + 1].at[flat_index(sizes, offsets)],
                grid.peer(me, stages[last], offsets[last]),
            ).wait_recv()
            used[at] = forward(at, stages, offsets, block, used[at])
    for copy in sent:
        copy.wait_send()
    for copy in own:
        copy.wait()


def gather_blocks(grid, identity, arrays, plans):
    scratch = []
    for stages in plans:
        scratch += [
            pltpu.SemaphoreType.DMA((gather_sends(grid, stages),)),
            pltpu.SemaphoreType.DMA((grid.count(stages),)),
            pltpu.SemaphoreType.DMA,
        ]
    bytes_moved = sum(
        2 * grid.count(stages) * array.size * array.dtype.itemsize
        for array, stages in zip(arrays, plans)
    )
    return pl.pallas_call(
        functools.partial(gather_kernel, grid, plans),
        out_shape=[
            jax.ShapeDtypeStruct((grid.count(stages), *array.shape), array.dtype)
            for array, stages in zip(arrays, plans)
        ],
        in_specs=[pl.BlockSpec(memory_space=pl.ANY)] * len(plans),
        out_specs=[pl.BlockSpec(memory_space=pl.ANY)] * len(plans),
        scratch_shapes=scratch,
        compiler_params=pltpu.CompilerParams(collective_id=identity, has_side_effects=True),
        cost_estimate=pl.CostEstimate(
            flops=0, bytes_accessed=bytes_moved * 8, transcendentals=0
        ),
        name=f"gather_blocks_{identity}",
    )(*arrays)


def rest_count(grid, stages, stage):
    return (grid.size[stages[stage]] - 1) * grid.count(stages[stage + 1 :])


def rest_index(grid, stages, stage, offsets):
    index = offsets[stage] - 1
    for at in range(stage + 1, len(stages)):
        index = index * grid.size[stages[at]] + offsets[at]
    return index


def scatter_kernel(grid, plans, with_gains, *refs):
    number = len(plans)
    extra = 1 if with_gains else 0
    sources = refs[: number + extra]
    targets = refs[number + extra : 2 * (number + extra)]
    scratch = list(refs[2 * (number + extra) :])
    me = grid.here()
    greet(
        grid,
        me,
        [
            axis
            for axis in SLOT_ORDER
            if with_gains or any(axis in stages for stages in plans)
        ],
    )
    sent = []
    tasks = []
    for stages in plans:
        landing, leaving, send, receive = [], [None], [], []
        for stage in range(len(stages)):
            landing.append(scratch.pop(0))
            if stage:
                leaving.append(scratch.pop(0))
            send.append(scratch.pop(0))
            receive.append(scratch.pop(0))
        tasks.append((landing, leaving, send, receive))

    def pick(at, stages, stage):
        choices = [[0]] * stage + [range(1, grid.size[stages[stage]])]
        for axis in stages[stage + 1 :]:
            choices.append([*range(1, grid.size[axis]), 0])
        later = list(itertools.product(*choices))
        return sorted(later, key=lambda offsets: [offset == 0 for offset in reversed(offsets)])

    def push(at, stages, stage, offsets, source):
        landing, leaving, send, receive = tasks[at]
        index = rest_index(grid, stages, stage, offsets)
        copy = remote(
            source,
            landing[stage].at[index],
            send[stage].at[index],
            receive[stage].at[index],
            grid.peer(me, stages[stage], offsets[stage]),
        )
        copy.start()
        sent.append(copy)

    def total(at, stages, stage, offsets):
        landing, leaving, send, receive = tasks[at]
        parts = []
        for before in range(stage):
            for step in range(1, grid.size[stages[before]]):
                place = list(offsets)
                place[before] = step
                index = rest_index(grid, stages, before, place)
                block = landing[before].at[index]
                remote(
                    block,
                    block,
                    send[before].at[index],
                    receive[before].at[index],
                    grid.peer(me, stages[before], step),
                ).wait_recv()
                parts.append(block)
        amount = sources[at][grid.slot(me, stages, offsets)].astype(jnp.float32)
        for block in parts:
            amount = amount + block[...].astype(jnp.float32)
        return amount

    for at, stages in enumerate(plans):
        for offsets in pick(at, stages, 0):
            push(at, stages, 0, offsets, sources[at].at[grid.slot(me, stages, offsets)])
    if with_gains:
        amount = sources[number][...]
        for axis in ("tensor", "shard", "lo", "hi"):
            held, send, receive = scratch.pop(0), scratch.pop(0), scratch.pop(0)
            held[me[axis]] = amount
            copies = []
            for step in range(1, grid.size[axis]):
                copy = remote(
                    held.at[me[axis]],
                    held.at[me[axis]],
                    send.at[step - 1],
                    receive.at[step - 1],
                    grid.peer(me, axis, step),
                )
                copy.start()
                copies.append(copy)
            for step in range(1, grid.size[axis]):
                block = held.at[(me[axis] - step) % grid.size[axis]]
                remote(
                    block,
                    block,
                    send.at[step - 1],
                    receive.at[step - 1],
                    grid.peer(me, axis, step),
                ).wait_recv()
            amount = held[0]
            for index in range(1, grid.size[axis]):
                amount = amount + held[index]
            sent += copies
        targets[number][...] = amount
    for stage in range(1, max(len(stages) for stages in plans)):
        everything = []
        for at, stages in enumerate(plans):
            if stage < len(stages):
                everything += [
                    (turn, at, offsets)
                    for turn, offsets in enumerate(pick(at, stages, stage))
                ]
        if everything:
            for turn, at, offsets in sorted(everything):
                stages = plans[at]
                leaving = tasks[at][1][stage].at[rest_index(grid, stages, stage, offsets)]
                leaving[...] = total(at, stages, stage, offsets).astype(leaving.dtype)
                push(at, stages, stage, offsets, leaving)
    for at, stages in enumerate(plans):
        targets[at][...] = total(at, stages, len(stages), (0,) * len(stages))
    for copy in sent:
        copy.wait_send()


def scatter_sums(grid, identity, arrays, plans, gains=None):
    scratch = []
    for array, stages in zip(arrays, plans):
        for stage in range(len(stages)):
            count = rest_count(grid, stages, stage)
            scratch.append(pltpu.VMEM((count, *array.shape[1:]), array.dtype))
            if stage:
                scratch.append(pltpu.VMEM((count, *array.shape[1:]), array.dtype))
            scratch += [pltpu.SemaphoreType.DMA((count,)), pltpu.SemaphoreType.DMA((count,))]
    outs = [jax.ShapeDtypeStruct(array.shape[1:], jnp.float32) for array in arrays]
    operands = list(arrays)
    if gains is not None:
        for axis in ("tensor", "shard", "lo", "hi"):
            size = grid.size[axis]
            scratch += [
                pltpu.VMEM((size, *gains.shape), gains.dtype),
                pltpu.SemaphoreType.DMA((max(size - 1, 1),)),
                pltpu.SemaphoreType.DMA((max(size - 1, 1),)),
            ]
        operands.append(gains)
        outs.append(jax.ShapeDtypeStruct(gains.shape, gains.dtype))
    bytes_moved = sum(2 * array.size * array.dtype.itemsize for array in arrays)
    return pl.pallas_call(
        functools.partial(scatter_kernel, grid, plans, gains is not None),
        out_shape=outs,
        in_specs=[pl.BlockSpec(memory_space=pltpu.VMEM)] * len(operands),
        out_specs=[pl.BlockSpec(memory_space=pltpu.VMEM)] * len(operands),
        scratch_shapes=scratch,
        compiler_params=pltpu.CompilerParams(
            collective_id=identity, has_side_effects=True, vmem_limit_bytes=VMEM_LIMIT
        ),
        cost_estimate=pl.CostEstimate(
            flops=0, bytes_accessed=bytes_moved * 8, transcendentals=0
        ),
        name=f"scatter_sums_{identity}",
    )(*operands)


def dot_last(left, right):
    return lax.dot_general(left, right, (((1,), (1,)), ((), ())), preferred_element_type=jnp.float32)


def dot_plain(left, right):
    return lax.dot_general(left, right, (((1,), (0,)), ((), ())), preferred_element_type=jnp.float32)


def dot_first(left, right):
    return lax.dot_general(left, right, (((0,), (0,)), ((), ())), preferred_element_type=jnp.float32)


def side_by_side(ref):
    return jnp.concatenate([ref[index] for index in range(ref.shape[0])], axis=1)


def spread(ref, amount):
    width = ref.shape[2]
    for index in range(ref.shape[0]):
        ref[index] = amount[:, index * width : (index + 1) * width].astype(ref.dtype)


def attend_kernel(queries, keys, values, bias, mixed, norms):
    scores = dot_first(side_by_side(keys), side_by_side(queries)) + bias[...]
    highest = jnp.max(scores, axis=0, keepdims=True)
    weights = jnp.exp(scores - highest)
    sums = jnp.sum(weights, axis=0, keepdims=True)
    probs = (weights * (1.0 / sums)).astype(jnp.bfloat16)
    spread(mixed, dot_plain(side_by_side(values), probs))
    norms[0] = highest + jnp.log(sums)


def attend_back_kernel(queries, keys, values, bias, norms, gradient, grad_q, grad_k, grad_v):
    all_queries, all_keys = side_by_side(queries), side_by_side(keys)
    all_gradients = side_by_side(gradient)
    scores = dot_first(all_keys, all_queries) + bias[...]
    probs = jnp.exp(scores - norms[0])
    grad_probs = dot_first(side_by_side(values), all_gradients)
    delta = jnp.sum(probs * grad_probs, axis=0, keepdims=True)
    grad_scores = (probs * (grad_probs - delta)).astype(jnp.bfloat16)
    spread(grad_q, dot_plain(all_keys, grad_scores) * HEAD_WIDTH ** (-0.5))
    spread(grad_k, dot_last(all_queries, grad_scores))
    spread(grad_v, dot_last(all_gradients, probs.astype(jnp.bfloat16)))


def group_spec(count):
    return pl.BlockSpec((GROUP, HEAD_WIDTH, count), lambda head: (head, 0, 0))


def pair_spec(blocks, count, shift):
    return pl.BlockSpec((blocks, HEAD_WIDTH, count), lambda head: (0, head + shift, 0))


def row_spec(rows):
    return pl.BlockSpec((1, 1, rows), lambda head: (head, 0, 0))


def attend(queries, pairs, bias):
    blocks, unused, count = pairs.shape
    rows = GROUP * count
    return pl.pallas_call(
        attend_kernel,
        grid=(KEY_VALUE_HEADS,),
        in_specs=[
            group_spec(count),
            pair_spec(blocks, count, 0),
            pair_spec(blocks, count, KEY_VALUE_HEADS),
            pl.BlockSpec(bias.shape, lambda head: (0, 0)),
        ],
        out_specs=[group_spec(count), row_spec(rows)],
        out_shape=[
            jax.ShapeDtypeStruct(queries.shape, jnp.bfloat16),
            jax.ShapeDtypeStruct((KEY_VALUE_HEADS, 1, rows), jnp.float32),
        ],
        compiler_params=pltpu.CompilerParams(vmem_limit_bytes=VMEM_LIMIT),
        name="attend",
    )(queries, pairs, pairs, bias)


def attend_back(queries, pairs, bias, norms, gradient):
    blocks, unused, count = pairs.shape
    rows = GROUP * count
    grad_pair = jax.ShapeDtypeStruct((blocks, KEY_VALUE_HEADS * HEAD_WIDTH, count), jnp.bfloat16)
    return pl.pallas_call(
        attend_back_kernel,
        grid=(KEY_VALUE_HEADS,),
        in_specs=[
            group_spec(count),
            pair_spec(blocks, count, 0),
            pair_spec(blocks, count, KEY_VALUE_HEADS),
            pl.BlockSpec(bias.shape, lambda head: (0, 0)),
            row_spec(rows),
            group_spec(count),
        ],
        out_specs=[
            group_spec(count),
            pair_spec(blocks, count, 0),
            pair_spec(blocks, count, 0),
        ],
        out_shape=[jax.ShapeDtypeStruct(queries.shape, jnp.float32), grad_pair, grad_pair],
        compiler_params=pltpu.CompilerParams(vmem_limit_bytes=VMEM_LIMIT),
        name="attend_back",
    )(queries, pairs, pairs, bias, norms, gradient)


def units_kernel(units, *refs):
    *pieces, cot, weights, grad_norm, unit_out, grads = refs
    blocks = pieces[0].shape[0]
    gate_w, up_w = weights[:units], weights[units : 2 * units]
    down_w = weights[2 * units :]
    rows = jnp.concatenate([piece[at] for at in range(blocks) for piece in pieces], axis=0)
    incoming = cot[...]
    gates, lifted = dot_last(rows, gate_w), dot_last(rows, up_w)
    grad_hidden = dot_last(incoming, down_w)
    sigmoid = jax.nn.sigmoid(gates)
    silu = gates * sigmoid
    hidden = (silu * lifted).astype(jnp.bfloat16)
    grad_gates = (grad_hidden * lifted * sigmoid * (1.0 + gates * (1.0 - sigmoid))).astype(
        jnp.bfloat16
    )
    grad_lifted = (grad_hidden * silu).astype(jnp.bfloat16)
    grad_norm[...] = (dot_plain(grad_gates, gate_w) + dot_plain(grad_lifted, up_w)).astype(
        grad_norm.dtype
    )
    unit_out[...] = dot_plain(hidden, down_w).astype(unit_out.dtype)

    @pl.when(pl.program_id(0) == 0)
    def clear():
        grads[...] = jnp.zeros_like(grads)

    grads[:units] += dot_first(grad_gates, rows)
    grads[units : 2 * units] += dot_first(grad_lifted, rows)
    grads[2 * units :] += dot_first(hidden, incoming)


def feed_forward(pieces, cot, weights):
    total, width = cot.shape
    blocks, height = 2, pieces[0].shape[1]
    rows = blocks * height * len(pieces)
    by_blocks = pl.BlockSpec((blocks, height, width), lambda step: (step, 0, 0))
    units = weights.shape[0] // 3
    by_rows = pl.BlockSpec((rows, width), lambda step: (step, 0))
    whole = pl.BlockSpec(weights.shape, lambda step: (0, 0))
    return pl.pallas_call(
        functools.partial(units_kernel, units),
        grid=(total // rows,),
        in_specs=[by_blocks] * len(pieces) + [by_rows, whole],
        out_specs=[by_rows, by_rows, whole],
        out_shape=[
            jax.ShapeDtypeStruct(cot.shape, jnp.bfloat16),
            jax.ShapeDtypeStruct(cot.shape, jnp.bfloat16),
            jax.ShapeDtypeStruct(weights.shape, jnp.float32),
        ],
        compiler_params=pltpu.CompilerParams(vmem_limit_bytes=VMEM_LIMIT),
        name="feed_forward",
    )(*pieces, cot, weights)


def rms_scale(value_matrix, gain):
    return (
        value_matrix
        * lax.rsqrt(jnp.mean(value_matrix * value_matrix, axis=-1, keepdims=True) + epsilon)
        * gain
    )


def apply_rotation(features, slot_positions, direction):
    half_dim = HEAD_WIDTH // 2
    freqs = 10000.0 ** (-jnp.arange(half_dim, dtype=jnp.float32) / half_dim)
    angles = freqs[:, None] * slot_positions.astype(jnp.float32)[None, :]
    cosine = jnp.cos(angles)[None]
    sine = direction * jnp.sin(angles)[None]
    heads = features.shape[0] // HEAD_WIDTH
    split_heads = features.reshape(heads, HEAD_WIDTH, features.shape[1])
    first_half = split_heads[:, :half_dim]
    second_half = split_heads[:, half_dim:]
    return jnp.concatenate(
        [first_half * cosine - second_half * sine, second_half * cosine + first_half * sine],
        axis=1,
    ).reshape(features.shape)


PIECES = 4
GATHER_PART = ("hi", "lo", "tensor")
GATHER_ALL = [("hi", "lo", "shard", "tensor"), ("hi", "shard", "lo", "tensor")]
SCATTER_PART = ("tensor", "lo", "hi")
SCATTER_ALL = [("tensor", "shard", "lo", "hi"), ("tensor", "lo", "shard", "hi")]


def body(
    grid,
    tokens,
    positions,
    gain_one,
    w_query,
    key_weight,
    value_weight,
    w_out,
    gain_two,
    w_gate,
    w_up,
    w_down,
    cotangent,
):
    shards = grid.size["shard"]
    devices = grid.count(GATHER_PART)
    inputs = tokens[0].astype(jnp.float32)
    slot_positions = positions[0]
    incoming = cotangent[0].astype(jnp.float32)
    count, width = inputs.shape
    part = width // shards
    q_rows, k_rows, units = w_query.shape[0], key_weight.shape[0], w_gate.shape[0]
    both = q_rows + k_rows
    kv_width = KEY_VALUE_HEADS * HEAD_WIDTH
    total_rows = devices * count
    flat = devices * both

    def columns(rows):
        return [rows[:, at * part : (at + 1) * part] for at in range(shards)]

    def sum_halves(weights, halves, dot):
        total = dot(weights[0], halves[0])
        for at in range(1, shards):
            total = total + dot(weights[at], halves[at])
        return total.reshape(devices, both, count)

    first_blocks, second_blocks = gather_blocks(
        grid,
        1,
        [
            jnp.concatenate([w_query, key_weight], axis=0),
            jnp.concatenate([value_weight, w_out], axis=0),
        ],
        GATHER_ALL,
    )
    first_blocks, own_cot = lax.optimization_barrier((first_blocks, cotangent[0]))
    cot_all = lax.all_gather(own_cot, ("context", "tensor"), axis=0, tiled=True)
    first_w = first_blocks.reshape(shards, flat, part)
    second_w = second_blocks.reshape(shards, flat, part)

    normed_one = rms_scale(inputs, gain_one).astype(jnp.bfloat16)
    normed_halves = columns(normed_one)
    first = sum_halves(first_w, normed_halves, dot_last)
    second = sum_halves(second_w, normed_halves, dot_last)
    queries = first[:, :q_rows].reshape(width, count)
    keys = first[:, q_rows:].reshape(kv_width, count)
    values = second[:, :k_rows].reshape(kv_width, count).astype(jnp.bfloat16)
    turned_q = apply_rotation(queries, slot_positions, 1.0).astype(jnp.bfloat16)
    turned_k = apply_rotation(keys, slot_positions, 1.0).astype(jnp.bfloat16)
    block_number = (slot_positions[0] // count).astype(jnp.bfloat16)
    pack = jnp.concatenate(
        [turned_k, values, jnp.broadcast_to(block_number, (16, count))], axis=0
    )
    units_w = jnp.concatenate([w_gate, w_up, w_down], axis=0)
    pairs, units_blocks = gather_blocks(grid, 2, [pack, units_w], [GATHER_PART, ("shard",)])
    block_numbers = pairs[:, 2 * kv_width, 0].astype(jnp.int32)
    key_places = (block_numbers[:, None] * count + jnp.arange(count)[None, :]).reshape(total_rows)
    query_places = jnp.tile(slot_positions, GROUP)
    bias = jnp.where(key_places[:, None] <= query_places[None, :], 0.0, -1e30).astype(jnp.float32)
    grouped_queries = (turned_q * jnp.bfloat16(HEAD_WIDTH ** (-0.5))).reshape(
        QUERY_HEAD_COUNT, HEAD_WIDTH, count
    )
    mixed, norms = attend(grouped_queries, pairs, bias)
    mixed_halves = mixed.reshape(shards, part, count)

    branch = sum_halves(second_w, mixed_halves, dot_plain)[:, k_rows:].reshape(width, count)
    middle = inputs + branch.T
    normed_two = rms_scale(middle, gain_two).astype(jnp.bfloat16)
    height = count // PIECES
    pieces = [normed_two[at * height : (at + 1) * height] for at in range(PIECES)]
    normed_pieces = gather_blocks(grid, 3, pieces, [GATHER_PART] * PIECES)
    units_full = units_blocks.transpose(1, 0, 2).reshape(3 * units, width)
    grad_norm_part, unit_part, grad_units = feed_forward(normed_pieces, cot_all, units_full)
    (grad_normed_two,) = scatter_sums(
        grid, 4, [grad_norm_part.reshape(devices, count, width)], [SCATTER_PART]
    )
    unit_part, grad_normed_two = lax.optimization_barrier((unit_part, grad_normed_two))
    unit_out = lax.psum_scatter(
        unit_part, ("context", "tensor"), scatter_dimension=0, tiled=True
    ).astype(jnp.float32)
    output = (middle + unit_out).astype(jnp.bfloat16)[None]

    unused_two, pull_two = jax.vjp(rms_scale, middle, gain_two)
    grad_middle_norm, grad_gain_two = pull_two(grad_normed_two)
    grad_middle = incoming + grad_middle_norm
    grad_branch = grad_middle.astype(jnp.bfloat16)
    blank_k = jnp.zeros((devices, k_rows, count), jnp.bfloat16)
    blank_q = jnp.zeros((devices, q_rows, count), jnp.bfloat16)
    grad_out_rows = jnp.concatenate(
        [blank_k, grad_branch.T.reshape(devices, q_rows, count)], axis=1
    ).reshape(flat, count)
    mixed_gradient = jnp.concatenate(
        [dot_first(second_w[at], grad_out_rows) for at in range(shards)], axis=0
    ).astype(jnp.bfloat16)
    query_gradient, grad_keys, grad_values = attend_back(
        grouped_queries, pairs, bias, norms, mixed_gradient.reshape(grouped_queries.shape)
    )
    grad_units = grad_units.astype(jnp.bfloat16).reshape(3 * units, shards, part)
    key_sum, value_sum, unit_sums = scatter_sums(
        grid,
        5,
        [grad_keys, grad_values, grad_units.transpose(1, 0, 2)],
        [SCATTER_PART, SCATTER_PART, ("shard",)],
    )
    grad_q = apply_rotation(query_gradient.reshape(width, count), slot_positions, -1.0)
    grad_k = apply_rotation(key_sum, slot_positions, -1.0)
    first_rows = jnp.concatenate(
        [
            grad_q.astype(jnp.bfloat16).reshape(devices, q_rows, count),
            grad_k.astype(jnp.bfloat16).reshape(devices, k_rows, count),
        ],
        axis=1,
    ).reshape(flat, count)
    value_rows = jnp.concatenate(
        [value_sum.astype(jnp.bfloat16).reshape(devices, k_rows, count), blank_q], axis=1
    ).reshape(flat, count)
    grad_normed_one = jnp.concatenate(
        [
            dot_first(first_rows, first_w[at]) + dot_first(value_rows, second_w[at])
            for at in range(shards)
        ],
        axis=1,
    )
    unused_one, pull_one = jax.vjp(rms_scale, inputs, gain_one)
    grad_inputs_norm, grad_gain_one = pull_one(grad_normed_one)
    grad_tokens = (grad_middle + grad_inputs_norm).astype(jnp.bfloat16)[None]
    first_grads = jnp.stack(
        [dot_plain(first_rows, half).astype(jnp.bfloat16) for half in normed_halves]
    )
    second_grads = jnp.stack(
        [
            (
                dot_plain(value_rows, normed_halves[at])
                + dot_last(grad_out_rows, mixed_halves[at])
            ).astype(jnp.bfloat16)
            for at in range(shards)
        ]
    )
    gains = jnp.zeros((8, width), jnp.float32).at[0].set(grad_gain_one).at[1].set(grad_gain_two)
    first_sums, second_sums, gain_sums = scatter_sums(
        grid,
        6,
        [
            first_grads.reshape(shards * devices, both, part),
            second_grads.reshape(shards * devices, both, part),
        ],
        SCATTER_ALL,
        gains,
    )
    return (
        output,
        grad_tokens,
        gain_sums[0],
        first_sums[:q_rows],
        first_sums[q_rows:],
        second_sums[:k_rows],
        second_sums[k_rows:],
        gain_sums[1],
        unit_sums[:units],
        unit_sums[units : 2 * units],
        unit_sums[2 * units :],
    )


def solution(mesh):
    placed = (
        P("shard", ("context", "tensor"), None),
        P("shard", ("context", "tensor")),
        P(),
        P(("context", "tensor"), "shard"),
        P(("context", "tensor"), "shard"),
        P(("context", "tensor"), "shard"),
        P(("context", "tensor"), "shard"),
        P(),
        P(("context", "tensor"), "shard"),
        P(("context", "tensor"), "shard"),
        P(("context", "tensor"), "shard"),
        P("shard", ("context", "tensor"), None),
    )
    return jax.shard_map(
        functools.partial(body, Grid(mesh)),
        mesh=mesh,
        in_specs=placed,
        out_specs=(
            P("shard", ("context", "tensor"), None),
            P("shard", ("context", "tensor"), None),
            P(),
            P(("context", "tensor"), "shard"),
            P(("context", "tensor"), "shard"),
            P(("context", "tensor"), "shard"),
            P(("context", "tensor"), "shard"),
            P(),
            P(("context", "tensor"), "shard"),
            P(("context", "tensor"), "shard"),
            P(("context", "tensor"), "shard"),
        ),
        check_vma=False,
    )
```
